32 devices in a mesh: grp: 2 (over y), slab: 4 (over x, core), row: 4 (over z).
Axes of the slice: x: 2, y: 2, z: 4, core: 2. Of those that a mesh axis runs over, the one named last changes fastest.
Arguments:
- velocity: float32 [3, 128, 16, 512], P(None, 'slab', 'grp', 'row'), may hold values from -6 to 6
- modes: float32 [24576, 512], P(('grp', 'slab', 'row')), may hold values from -6 to 6
- planes: int32 [64], replicated, may hold values from 0 to 127, as said below
- assign: int32 [4], replicated, may hold values from 0 to 3, each once
Outputs:
- advanced: float32 [3, 128, 16, 512], P(None, 'slab', 'grp', 'row')
- basis: float32 [24576, 576], P(('grp', 'slab', 'row'))
- factor: float32 [576, 576], replicated
The draws below stay inside these ranges and needn't reach their ends.
Inputs may be any that keep to these rules, and one draw needn't show every extreme that they name: `planes`: the 64 plane indices are distinct.
All inputs are finite; a program needn't handle non-finite values.
Results may differ from the reference program's by a relative error of at most 0.00005.
Values sent between devices are 32-bit elements; how exact they have to be, the bound alone decides.
A program may use at most 64 MiB of HBM per device.

```python
import jax
import jax.numpy as jnp
from jax import lax

CX = 8
CY = 128
NSNAP = 64
RANK = 512
NX = 16
NY = 512
NZ = 128
BLK = 768
ROWS = 24576
N_GRP = 2
N_SLAB = 4
N_ROW = 4


def draw_planes(key, part):
    keys = jax.random.split(jax.random.fold_in(key, 17), 2)
    others = jnp.concatenate([jnp.arange(NSNAP - 1, dtype=jnp.int32), jnp.arange(NSNAP + 1, 2 * NSNAP, dtype=jnp.int32)])
    chosen = others[jax.random.permutation(keys[0], 2 * NSNAP - 2)[:NSNAP - 2]]
    offsets = jnp.concatenate([chosen, jnp.array([NSNAP - 1, NSNAP], dtype=jnp.int32)])
    offsets = offsets[jax.random.permutation(keys[1], NSNAP)]
    return ((NZ - NSNAP + offsets) % NZ).astype(jnp.int32)


def block_levels(stream_key, extent, pieces, least, high):
    def one(position, blocks):
        steps = jax.random.uniform(jax.random.fold_in(jax.random.fold_in(stream_key, 6), position), (blocks,), jnp.float32, least / len(pieces), high / len(pieces))
        return jnp.repeat(jnp.exp(steps), extent[position] // blocks).reshape((-1,) + (1,) * (len(extent) - position - 1))

    level = one(*pieces[0])
    for cut in pieces[1:]:
        level = level * one(*cut)
    return level


def gaussian(rng, extent, scale, reach, shards=(), kind=jnp.bfloat16):
    values = scale * jax.random.normal(rng, extent, jnp.float32)
    if shards:
        values = values * block_levels(rng, extent, shards, -0.22, 0.18)
    return jnp.clip(values, -reach, reach).astype(kind)


def setup_inputs(seed: int = 0) -> dict:
    arg_keys = jax.random.split(jax.random.key(seed), 5)
    return {
        "velocity": gaussian(arg_keys[0], (3, NZ, NX, NY), 1.0, 6.0, ((1, 4), (2, 2), (3, 4)), jnp.float32),
        "modes": gaussian(arg_keys[1], (ROWS, RANK), 1.0, 6.0, ((0, 32),), jnp.float32),
        "planes": draw_planes(jax.random.fold_in(arg_keys[4], 71), 0),
        "assign": jax.random.permutation(arg_keys[3], N_SLAB).astype(jnp.int32),
    }


step_size = 0.05
viscosity = 1.0
third = 1.0 / 3.0
carry_back = -5.0 / 9.0
second_gain = 15.0 / 16.0

def derivatives(parts):
    first = (parts[0] - 8.0 * parts[1] + 8.0 * parts[3] - parts[4]) / 12.0
    second = (-parts[0] + 16.0 * parts[1] - 30.0 * parts[2] + 16.0 * parts[3] - parts[4]) / 12.0
    return (first, second)

def periodic_parts(field, dim):
    return [jnp.roll(field, 2 - k, axis=dim) for k in range(5)]

def wall_parts(field, dim):
    length = field.shape[dim]
    widths = [(0, 0)] * field.ndim
    widths[dim] = (2, 2)
    padded = jnp.pad(field, widths)
    return [lax.slice_in_dim(padded, k, k + length, axis=dim) for k in range(5)]

def tendency(along_z, along_x, along_y, field):
    dz_first, dz_second = derivatives(along_z)
    dx_first, dx_second = derivatives(along_x)
    dy_first, dy_second = derivatives(along_y)
    convect = field[0:1] * dx_first + field[1:2] * dy_first + field[2:3] * dz_first
    laplace = dx_second + dy_second + dz_second
    return viscosity * laplace - convect

def whole_tendency(field):
    return tendency(periodic_parts(field, 1), periodic_parts(field, 2), wall_parts(field, 3), field)

def reference(velocity, modes, planes, assign):
    first_q = step_size * whole_tendency(velocity)
    middle = velocity + third * first_q
    second_q = carry_back * first_q + step_size * whole_tendency(middle)
    advanced = middle + second_gain * second_q
    picked = jnp.take(advanced, planes, axis=1)
    picked = jnp.transpose(picked, (1, 0, 2, 3)).reshape(NSNAP, 3, N_GRP, CX, N_ROW, CY)
    picked = jnp.transpose(picked, (0, 2, 4, 1, 3, 5)).reshape(NSNAP, N_GRP, N_ROW, N_SLAB, BLK)
    picked = jnp.take(picked, assign, axis=3)
    snapshot_block = jnp.transpose(picked, (1, 3, 2, 4, 0)).reshape(ROWS, NSNAP)
    joined = jnp.concatenate([modes, snapshot_block], axis=1)
    gram = jnp.dot(joined.T.astype(jnp.float32), joined.astype(jnp.float32), precision=lax.Precision.HIGHEST, preferred_element_type=jnp.float32) / float(ROWS)
    lower = jnp.linalg.cholesky(gram)
    basis = jax.scipy.linalg.solve_triangular(lower, joined.T, lower=True).T
    return (advanced, basis, lower.T)
```

```python
import functools

import jax
import jax.numpy as jnp
from jax import lax
from jax.experimental import pallas as pl
from jax.experimental.pallas import tpu as pltpu
from jax.sharding import PartitionSpec as P

step_size = 0.05
viscosity = 1.0
third = 1.0 / 3.0
carry_back = -5.0 / 9.0
second_gain = 15.0 / 16.0
EDGE = 128
PANEL = 8


def padded(array, sides, width, wrap):
    for axis, dim in sides:
        devices, length = (lax.axis_size(axis), array.shape[dim])
        up = [(i, (i + 1) % devices) for i in range(devices if wrap else devices - 1)]
        down = [(j, i) for i, j in up]
        last = lax.slice_in_dim(array, length - width, length, axis=dim)
        initial = lax.slice_in_dim(array, 0, width, axis=dim)
        before = lax.ppermute(last, axis, up)
        after = lax.ppermute(initial, axis, down)
        array = jnp.concatenate([before, array, after], axis=dim)
    return array


def derivatives(parts):
    first = (parts[0] - 8.0 * parts[1] + 8.0 * parts[3] - parts[4]) / 12.0
    second = (-parts[0] + 16.0 * parts[1] - 30.0 * parts[2] + 16.0 * parts[3] - parts[4]) / 12.0
    return (first, second)


def tendency(field):
    wide = padded(field, (("grp", 2), ("slab", 1)), 2, True)
    walls = padded(field, (("row", 3),), 2, False)
    depth, across, height = (field.shape[1], field.shape[2], field.shape[3])
    along_z = [wide[:, k : k + depth, 2 : 2 + across, :] for k in range(5)]
    along_x = [wide[:, 2 : 2 + depth, k : k + across, :] for k in range(5)]
    along_y = [walls[:, :, :, k : k + height] for k in range(5)]
    dz_first, dz_second = derivatives(along_z)
    dx_first, dx_second = derivatives(along_x)
    dy_first, dy_second = derivatives(along_y)
    convect = field[0:1] * dx_first + field[1:2] * dy_first + field[2:3] * dz_first
    laplace = dx_second + dy_second + dz_second
    return viscosity * laplace - convect


def product(left, right, dims=((1,), (0,))):
    return lax.dot_general(
        left, right, (dims, ((), ())),
        precision=lax.Precision.HIGHEST, preferred_element_type=jnp.float32,
    )


def eliminate(tile, factor_ref, inverse_ref):
    size = tile.shape[0]
    lane = lax.broadcasted_iota(jnp.int32, (PANEL, size), 1)
    sub = lax.broadcasted_iota(jnp.int32, (PANEL, size), 0)
    groups = [tile[PANEL * g : PANEL * (g + 1), :] for g in range(size // PANEL)]
    for p in range(size // PANEL):
        start = PANEL * p
        own = groups[p]
        inside = (lane >= start) & (lane < start + PANEL)
        columns = [
            jnp.broadcast_to(own[:, start + k : start + k + 1], own.shape) for k in range(PANEL)
        ]
        direct = own
        unit = jnp.where(inside, jnp.where(lane - start == sub, 1.0, 0.0), own)
        factor_rows = jnp.zeros_like(own)
        inverse_rows = jnp.zeros_like(own)
        for k in range(PANEL):
            pivot = columns[k][k : k + 1, :]
            root = lax.rsqrt(pivot)
            scale = 1.0 / pivot
            here = sub == k
            row_direct, row_unit = direct[k : k + 1, :], unit[k : k + 1, :]
            factor_rows = jnp.where(here, row_direct * root, factor_rows)
            inverse_rows = jnp.where(here, row_unit * root, inverse_rows)
            others = jnp.where(here, 0.0, columns[k])
            for j in range(k + 1, PANEL):
                row = columns[j][k : k + 1, :] * scale
                columns[j] = jnp.where(here, row, columns[j]) - others * row
            row = row_direct * scale
            direct = jnp.where(here, row, direct) - others * row
            row = row_unit * scale
            unit = jnp.where(here, row, unit) - others * row
        factor_ref[start : start + PANEL, :] = jnp.where(lane >= start + sub, factor_rows, 0.0)
        inverse_ref[start : start + PANEL, :] = jnp.where(lane <= start + sub, inverse_rows, 0.0)
        for g in range(p + 1, size // PANEL):
            below = groups[g]
            total = jnp.where(inside, 0.0, below)
            for k in range(PANEL):
                total = total - below[:, start + k : start + k + 1] * unit[k : k + 1, :]
            groups[g] = total


def factor_kernel(gram_ref, joined_ref, basis_ref, factor_ref, work, left, tile, upper, lower):
    size = gram_ref.shape[0]
    whole = work.shape[0]
    blocks = whole // EDGE
    work[...] = jnp.zeros_like(work)
    work[:size, :size] = gram_ref[...]
    tail = (blocks - 1) * EDGE
    row = lax.broadcasted_iota(jnp.int32, (EDGE, EDGE), 0)
    col = lax.broadcasted_iota(jnp.int32, (EDGE, EDGE), 1)
    padding = (row == col) & (row + tail >= size)
    work[tail:, tail:] = jnp.where(padding, 1.0, work[tail:, tail:])
    left[...] = jnp.zeros_like(left)
    left[:, :size] = joined_ref[...]
    factor_ref[...] = jnp.zeros_like(factor_ref)

    def step(k, carry):
        for b in range(blocks):
            @pl.when(k == b)
            def _():
                tile[...] = work[b * EDGE : (b + 1) * EDGE, b * EDGE : (b + 1) * EDGE]

        eliminate(tile[...], upper, lower)
        for b in range(blocks):
            @pl.when(k == b)
            def _():
                low, high = b * EDGE, (b + 1) * EDGE
                end = min(high, size)
                inverse = lower[...]
                solved = product(left[:, low:high], inverse, ((1,), (1,)))
                basis_ref[:, low:end] = solved[:, : end - low]
                factor_ref[low:end, low:end] = upper[: end - low, : end - low]
                if high < whole:
                    strip = product(inverse, work[low:high, high:])
                    factor_ref[low:high, high:] = strip[:, : size - high]
                    work[high:, high:] = work[high:, high:] - product(strip, strip, ((0,), (0,)))
                    left[:, high:] = left[:, high:] - product(solved, strip)

        return carry

    lax.fori_loop(0, blocks, step, 0)


def factorize(gram, joined):
    size = gram.shape[0]
    rows = joined.shape[0]
    whole = -(-size // EDGE) * EDGE
    vmem = pl.BlockSpec(memory_space=pltpu.VMEM)
    return pl.pallas_call(
        factor_kernel,
        out_shape=(
            jax.ShapeDtypeStruct((rows, size), jnp.float32),
            jax.ShapeDtypeStruct((size, size), jnp.float32),
        ),
        in_specs=[vmem, vmem],
        out_specs=(vmem, vmem),
        scratch_shapes=[
            pltpu.VMEM((whole, whole), jnp.float32),
            pltpu.VMEM((rows, whole), jnp.float32),
            pltpu.VMEM((EDGE, EDGE), jnp.float32),
            pltpu.VMEM((EDGE, EDGE), jnp.float32),
            pltpu.VMEM((EDGE, EDGE), jnp.float32),
        ],
        compiler_params=pltpu.CompilerParams(vmem_limit_bytes=40 * 1024 * 1024),
        name="factorize",
    )(gram, joined)


def on_device(velocity, modes, planes, assign):
    count = planes.shape[0]
    slabs = lax.axis_size("slab")
    rows_total = modes.shape[0] * lax.axis_size("grp") * slabs * lax.axis_size("row")
    first_q = step_size * tendency(velocity)
    middle = velocity + third * first_q
    second_q = carry_back * first_q + step_size * tendency(middle)
    advanced = middle + second_gain * second_q
    depth = velocity.shape[1]
    local_z = planes - lax.axis_index("slab") * depth
    owned = (local_z >= 0) & (local_z < depth)
    picked = jnp.take(advanced, jnp.clip(local_z, 0, depth - 1), axis=1)
    picked = jnp.where(owned[None, :, None, None], picked, 0.0)
    picked = jnp.transpose(picked, (1, 0, 2, 3)).reshape(count, slabs, -1)
    arranged = jnp.take(picked, assign, axis=1)
    received = lax.psum_scatter(
        arranged.reshape(count, -1), "slab", scatter_dimension=1, tiled=True
    )
    snapshot_rows = received.T
    joined = jnp.concatenate([modes, snapshot_rows], axis=1)
    summed = lax.psum(product(joined.T, joined), ("grp", "slab", "row"))
    gram = summed / float(rows_total)
    basis, factor = factorize(gram, joined)
    return (advanced, basis, factor)


def solution(mesh):
    placed = (P(None, "slab", "grp", "row"), P(("grp", "slab", "row"), None), P(), P())
    return jax.shard_map(
        on_device,
        mesh=mesh,
        in_specs=placed,
        out_specs=(P(None, "slab", "grp", "row"), P(("grp", "slab", "row"), None), P()),
        check_vma=False,
    )
```

```python
import functools

import jax
import jax.numpy as jnp
from jax import lax
from jax.experimental import pallas as pl
from jax.experimental.pallas import tpu as pltpu
from jax.sharding import PartitionSpec as P

step_size = 0.05
viscosity = 1.0
third = 1.0 / 3.0
carry_back = -5.0 / 9.0
second_gain = 15.0 / 16.0
EDGE = 128
PANEL = 8


def padded(array, sides, width, wrap):
    for axis, dim in sides:
        devices, length = (lax.axis_size(axis), array.shape[dim])
        up = [(i, (i + 1) % devices) for i in range(devices if wrap else devices - 1)]
        down = [(j, i) for i, j in up]
        last = lax.slice_in_dim(array, length - width, length, axis=dim)
        initial = lax.slice_in_dim(array, 0, width, axis=dim)
        before = lax.ppermute(last, axis, up)
        after = lax.ppermute(initial, axis, down)
        array = jnp.concatenate([before, array, after], axis=dim)
    return array


def derivatives(parts):
    first = (parts[0] - 8.0 * parts[1] + 8.0 * parts[3] - parts[4]) / 12.0
    second = (-parts[0] + 16.0 * parts[1] - 30.0 * parts[2] + 16.0 * parts[3] - parts[4]) / 12.0
    return (first, second)


def tendency(field):
    wide = padded(field, (("grp", 2), ("slab", 1)), 2, True)
    walls = padded(field, (("row", 3),), 2, False)
    depth, across, height = (field.shape[1], field.shape[2], field.shape[3])
    along_z = [wide[:, k : k + depth, 2 : 2 + across, :] for k in range(5)]
    along_x = [wide[:, 2 : 2 + depth, k : k + across, :] for k in range(5)]
    along_y = [walls[:, :, :, k : k + height] for k in range(5)]
    dz_first, dz_second = derivatives(along_z)
    dx_first, dx_second = derivatives(along_x)
    dy_first, dy_second = derivatives(along_y)
    convect = field[0:1] * dx_first + field[1:2] * dy_first + field[2:3] * dz_first
    laplace = dx_second + dy_second + dz_second
    return viscosity * laplace - convect


def product(left, right, dims=((1,), (0,))):
    return lax.dot_general(
        left, right, (dims, ((), ())),
        precision=lax.Precision.HIGHEST, preferred_element_type=jnp.float32,
    )


def eliminate(tile, factor_ref, inverse_ref):
    size = tile.shape[0]
    lane = lax.broadcasted_iota(jnp.int32, (PANEL, size), 1)
    sub = lax.broadcasted_iota(jnp.int32, (PANEL, size), 0)
    groups = [tile[PANEL * g : PANEL * (g + 1), :] for g in range(size // PANEL)]
    for p in range(size // PANEL):
        start = PANEL * p
        own = groups[p]
        inside = (lane >= start) & (lane < start + PANEL)
        columns = [
            jnp.broadcast_to(own[:, start + k : start + k + 1], own.shape) for k in range(PANEL)
        ]
        direct = own
        unit = jnp.where(inside, jnp.where(lane - start == sub, 1.0, 0.0), own)
        factor_rows = jnp.zeros_like(own)
        inverse_rows = jnp.zeros_like(own)
        for k in range(PANEL):
            pivot = columns[k][k : k + 1, :]
            root = lax.rsqrt(pivot)
            scale = 1.0 / pivot
            here = sub == k
            row_direct, row_unit = direct[k : k + 1, :], unit[k : k + 1, :]
            factor_rows = jnp.where(here, row_direct * root, factor_rows)
            inverse_rows = jnp.where(here, row_unit * root, inverse_rows)
            others = jnp.where(here, 0.0, columns[k])
            for j in range(k + 1, PANEL):
                row = columns[j][k : k + 1, :] * scale
                columns[j] = jnp.where(here, row, columns[j]) - others * row
            row = row_direct * scale
            direct = jnp.where(here, row, direct) - others * row
            row = row_unit * scale
            unit = jnp.where(here, row, unit) - others * row
        factor_ref[start : start + PANEL, :] = jnp.where(lane >= start + sub, factor_rows, 0.0)
        inverse_ref[start : start + PANEL, :] = jnp.where(lane <= start + sub, inverse_rows, 0.0)
        for g in range(p + 1, size // PANEL):
            below = groups[g]
            total = jnp.where(inside, 0.0, below)
            for k in range(PANEL):
                total = total - below[:, start + k : start + k + 1] * unit[k : k + 1, :]
            groups[g] = total


def wire_stages():
    slabs = lax.axis_size("slab")
    inner = 2 if slabs % 2 == 0 else 1
    parts = [("slab", inner, slabs // inner), ("grp", 1, lax.axis_size("grp")), ("row", 1, lax.axis_size("row"))]
    first = [("slab", 1, inner)]
    return [first + parts[k:] + parts[:k] for k in range(3)]


def place(stage):
    axis, stride, members = stage
    return lax.rem(lax.axis_index(axis) // stride, members)


def peer(stage, distance):
    axis, stride, members = stage
    mine = place(stage)
    other = lax.rem(mine + distance, members)
    return {axis: lax.axis_index(axis) + (other - mine) * stride}, other


def chunk_plan(rows, devices):
    unit = PANEL * devices
    units = rows // unit
    orders = wire_stages()
    chunks, base = [], 0
    for c in range(3):
        share = (units - sum(n for _, n, _ in chunks) + 2 - c) // (3 - c)
        if share:
            chunks.append((base * unit, share, orders[c]))
            base += share
    return [(start, share * unit, order) for start, share, order in chunks]


def inbox_rows(chunks):
    total = 0
    for _, length, order in chunks:
        for _, _, members in order:
            length //= members
            total += (members - 1) * length
    return total


def wire_count(chunks):
    return 2 * sum(members - 1 for _, _, order in chunks for _, _, members in order)


def combine_kernel(chunks, swap, *refs):
    if swap:
        part_ref, mine_ref, sum_ref, got_ref, acc, full, inbox, send, recv, got, swap_send, swap_recv = refs
    else:
        part_ref, sum_ref, acc, full, inbox, send, recv = refs
    barrier = pltpu.get_barrier_semaphore()
    stages = chunks[0][2]
    slab = ("slab", 1, lax.axis_size("slab"))
    greeted = [slab] + [st for st in stages if st[0] != "slab"] if swap else stages
    total = 0
    for stage in greeted:
        for d in range(1, stage[2]):
            pl.semaphore_signal(barrier, inc=1, device_id=peer(stage, d)[0], device_id_type=pl.DeviceIdType.MESH)
            total += 1
    acc[...] = part_ref[...]
    pl.semaphore_wait(barrier, total)

    count = 0
    slot = 0
    pending = []

    def begin(source, target, device, index):
        copy = pltpu.make_async_remote_copy(
            src_ref=source, dst_ref=target, send_sem=send.at[index], recv_sem=recv.at[index],
            device_id=device, device_id_type=pl.DeviceIdType.MESH,
        )
        copy.start()
        pending.append(copy)
        return copy

    offsets = [jnp.int32(base) for base, _, _ in chunks]
    lengths = [length for _, length, _ in chunks]
    trail = [[] for _ in chunks]
    swaps = []
    for s in range(len(stages)):
        started = []
        for c, (_, _, order) in enumerate(chunks):
            stage = order[s]
            piece = lengths[c] // stage[2]
            for d in range(1, stage[2]):
                device, other = peer(stage, d)
                source = acc.at[pl.ds(pl.multiple_of(offsets[c] + other * piece, PANEL), piece), :]
                copy = begin(source, inbox.at[pl.ds(slot, piece), :], device, count)
                started.append((c, copy, slot, piece))
                count += 1
                slot += piece
        if swap and s == 0:
            me = lax.axis_index("slab")
            for d in range(1, slab[2]):
                device, other = peer(slab, d)
                copy = pltpu.make_async_remote_copy(
                    src_ref=mine_ref.at[other], dst_ref=got.at[me],
                    send_sem=swap_send.at[d - 1], recv_sem=swap_recv.at[d - 1],
                    device_id=device, device_id_type=pl.DeviceIdType.MESH,
                )
                copy.start()
                swaps.append(copy)
        for c, (_, _, order) in enumerate(chunks):
            stage = order[s]
            piece = lengths[c] // stage[2]
            trail[c].append((offsets[c], lengths[c]))
            offsets[c] = pl.multiple_of(offsets[c] + place(stage) * piece, PANEL)
            lengths[c] = piece
            rows = pl.ds(offsets[c], piece)
            for owner, copy, where, size in started:
                if owner == c:
                    copy.wait_recv()
                    acc[rows, :] = acc[rows, :] + inbox[pl.ds(where, size), :]
    for c in range(len(chunks)):
        rows = pl.ds(offsets[c], lengths[c])
        full[rows, :] = acc[rows, :]
    for s in reversed(range(len(stages))):
        started = []
        for c, (_, _, order) in enumerate(chunks):
            stage = order[s]
            rows = pl.ds(offsets[c], lengths[c])
            for d in range(1, stage[2]):
                started.append(begin(full.at[rows, :], full.at[rows, :], peer(stage, d)[0], count))
                count += 1
            offsets[c], lengths[c] = trail[c][s]
            offsets[c] = pl.multiple_of(offsets[c], PANEL)
        for copy in started:
            copy.wait_recv()
    sum_ref[...] = full[...]
    if swap:
        for copy in swaps:
            copy.wait_recv()
        for j in range(slab[2]):
            @pl.when(lax.axis_index("slab") == j)
            def _():
                got_ref[j] = mine_ref[j]

            @pl.when(lax.axis_index("slab") != j)
            def _():
                got_ref[j] = got[j]
    for copy in pending + swaps:
        copy.wait_send()


def combine(part, mine, collective_id):
    devices = lax.axis_size("grp") * lax.axis_size("slab") * lax.axis_size("row")
    chunks = chunk_plan(part.shape[0], devices)
    swap = mine is not None
    wires = wire_count(chunks)
    vmem = pl.BlockSpec(memory_space=pltpu.VMEM)
    out = [jax.ShapeDtypeStruct(part.shape, jnp.float32)]
    scratch = [
        pltpu.VMEM(part.shape, jnp.float32),
        pltpu.VMEM(part.shape, jnp.float32),
        pltpu.VMEM((inbox_rows(chunks), EDGE), jnp.float32),
        pltpu.SemaphoreType.DMA((wires,)),
        pltpu.SemaphoreType.DMA((wires,)),
    ]
    operands = [part]
    if swap:
        operands.append(mine)
        out.append(jax.ShapeDtypeStruct(mine.shape, jnp.float32))
        scratch += [
            pltpu.VMEM(mine.shape, jnp.float32),
            pltpu.SemaphoreType.DMA((mine.shape[0] - 1,)),
            pltpu.SemaphoreType.DMA((mine.shape[0] - 1,)),
        ]
    return pl.pallas_call(
        functools.partial(combine_kernel, chunks, swap),
        out_shape=out,
        in_specs=[vmem] * len(operands),
        out_specs=[vmem] * len(out),
        scratch_shapes=scratch,
        compiler_params=pltpu.CompilerParams(
            collective_id=collective_id, has_side_effects=True, vmem_limit_bytes=40 * 1024 * 1024
        ),
        name=f"combine_{collective_id}",
    )(*operands)


def round_up(value, unit):
    return -(-value // unit) * unit


def modes_gram_kernel(modes_ref, out_ref):
    blocks = modes_ref.shape[1] // EDGE
    at = 0
    for i in range(blocks):
        strip = product(modes_ref[:, i * EDGE : (i + 1) * EDGE], modes_ref[:, i * EDGE :], ((0,), (0,)))
        for j in range(blocks - i):
            out_ref[at : at + EDGE, :] = strip[:, j * EDGE : (j + 1) * EDGE]
            at += EDGE
    if at < out_ref.shape[0]:
        out_ref[at:, :] = jnp.zeros((out_ref.shape[0] - at, EDGE), jnp.float32)


def snapshot_gram_kernel(count, planes_ref, got_ref, modes_ref, rows_ref, out_ref):
    held = got_ref.shape[0]
    cells = lax.broadcasted_iota(jnp.int32, (EDGE, held), 1)
    chosen = jnp.where(cells == planes_ref[...], 1.0, 0.0)
    rows_ref[...] = product(chosen, got_ref[...])
    snapshots = rows_ref[...]
    blocks = modes_ref.shape[1] // EDGE
    cross = product(snapshots[:count, :], modes_ref[...])
    for i in range(blocks):
        out_ref[i * count : (i + 1) * count, :] = cross[:, i * EDGE : (i + 1) * EDGE]
    out_ref[blocks * count : (blocks + 1) * count, :] = product(snapshots[:count, :], snapshots, ((1,), (1,)))
    at = (blocks + 1) * count
    if at < out_ref.shape[0]:
        out_ref[at:, :] = jnp.zeros((out_ref.shape[0] - at, EDGE), jnp.float32)


def factor_kernel(count, rows_total, first_ref, second_ref, modes_ref, rows_ref, basis_ref, factor_ref,
                  work, left, tile, upper, lower):
    rank = modes_ref.shape[1]
    size = rank + count
    whole = work.shape[0]
    blocks = whole // EDGE
    scale = 1.0 / rows_total
    at = 0
    for i in range(blocks - 1):
        low = i * EDGE
        for j in range(i, blocks - 1):
            work[low : low + EDGE, j * EDGE : (j + 1) * EDGE] = first_ref[at : at + EDGE, :] * scale
            at += EDGE
        cross = jnp.concatenate(
            [second_ref[i * count : (i + 1) * count, :], jnp.zeros((EDGE - count, EDGE), jnp.float32)], axis=0
        )
        work[low : low + EDGE, rank:] = cross.T * scale
    row = lax.broadcasted_iota(jnp.int32, (EDGE, EDGE), 0)
    col = lax.broadcasted_iota(jnp.int32, (EDGE, EDGE), 1)
    inner = second_ref[(blocks - 1) * count : blocks * count, :] * scale
    work[rank : rank + count, rank:] = inner
    work[rank + count :, rank:] = jnp.where((row == col) & (row >= count), 1.0, 0.0)[count:, :]
    left[:, :rank] = modes_ref[...]
    left[:, rank:] = rows_ref[...].T
    factor_ref[...] = jnp.zeros_like(factor_ref)

    def step(k, carry):
        for b in range(blocks):
            @pl.when(k == b)
            def _():
                tile[...] = work[b * EDGE : (b + 1) * EDGE, b * EDGE : (b + 1) * EDGE]

        eliminate(tile[...], upper, lower)
        for b in range(blocks):
            @pl.when(k == b)
            def _():
                low, high = b * EDGE, (b + 1) * EDGE
                end = min(high, size)
                inverse = lower[...]
                solved = product(left[:, low:high], inverse, ((1,), (1,)))
                basis_ref[:, low:end] = solved[:, : end - low]
                factor_ref[low:end, low:end] = upper[: end - low, : end - low]
                if high < whole:
                    strip = product(inverse, work[low:high, high:])
                    factor_ref[low:high, high:] = strip[:, : size - high]
                    work[high:, high:] = work[high:, high:] - product(strip, strip, ((0,), (0,)))
                    left[:, high:] = left[:, high:] - product(solved, strip)

        return carry

    lax.fori_loop(0, blocks, step, 0)


def plain(kernel, out_shape, scratch, name, *operands):
    vmem = pl.BlockSpec(memory_space=pltpu.VMEM)
    shapes = [jax.ShapeDtypeStruct(shape, jnp.float32) for shape in out_shape]
    return pl.pallas_call(
        kernel,
        out_shape=shapes,
        in_specs=[vmem] * len(operands),
        out_specs=[vmem] * len(shapes),
        scratch_shapes=[pltpu.VMEM(shape, jnp.float32) for shape in scratch],
        compiler_params=pltpu.CompilerParams(vmem_limit_bytes=40 * 1024 * 1024),
        name=name,
    )(*operands)


def decompose(advanced, modes, planes, assign):
    count = planes.shape[0]
    slabs = lax.axis_size("slab")
    devices = lax.axis_size("grp") * slabs * lax.axis_size("row")
    rows, rank = modes.shape
    size = rank + count
    whole = rank + EDGE
    depth = advanced.shape[1]
    unit = PANEL * devices
    blocks = rank // EDGE
    (first,) = plain(modes_gram_kernel, [(round_up(blocks * (blocks + 1) // 2 * EDGE, unit), EDGE)], [],
                     "modes_gram", modes)
    pieces = jnp.transpose(advanced, (1, 0, 2, 3)).reshape(depth, slabs, -1)
    mine = jnp.transpose(jnp.take(pieces, assign, axis=1, mode="clip"), (1, 0, 2))
    first, got = combine(first, mine, 0)
    chosen = jnp.pad(planes, (0, EDGE - count), constant_values=-1).reshape(EDGE, 1)
    snapshots, second = plain(
        functools.partial(snapshot_gram_kernel, count),
        [(EDGE, rows), (round_up((blocks + 1) * count, unit), EDGE)], [], "snapshot_gram",
        chosen, got.reshape(slabs * depth, rows), modes,
    )
    (second,) = combine(second, None, 1)
    return plain(
        functools.partial(factor_kernel, count, float(rows * devices)),
        [(rows, size), (size, size)],
        [(whole, whole), (rows, whole), (EDGE, EDGE), (EDGE, EDGE), (EDGE, EDGE)],
        "factorize", first, second, modes, snapshots,
    )


def on_device(velocity, modes, planes, assign):
    first_q = step_size * tendency(velocity)
    middle = velocity + third * first_q
    second_q = carry_back * first_q + step_size * tendency(middle)
    advanced = middle + second_gain * second_q
    basis, factor = decompose(advanced, modes, planes, assign)
    return (advanced, basis, factor)


def solution(mesh):
    placed = (P(None, "slab", "grp", "row"), P(("grp", "slab", "row"), None), P(), P())
    return jax.shard_map(
        on_device,
        mesh=mesh,
        in_specs=placed,
        out_specs=(P(None, "slab", "grp", "row"), P(("grp", "slab", "row"), None), P()),
        check_vma=False,
    )
```

```python
import functools

import jax
import jax.numpy as jnp
from jax import lax
from jax.experimental import pallas as pl
from jax.experimental.pallas import tpu as pltpu
from jax.sharding import PartitionSpec as P

step_size = 0.05
viscosity = 1.0
third = 1.0 / 3.0
carry_back = -5.0 / 9.0
second_gain = 15.0 / 16.0
EDGE = 128
PANEL = 8


def padded(array, sides, width, wrap):
    for axis, dim in sides:
        devices, length = (lax.axis_size(axis), array.shape[dim])
        up = [(i, (i + 1) % devices) for i in range(devices if wrap else devices - 1)]
        down = [(j, i) for i, j in up]
        last = lax.slice_in_dim(array, length - width, length, axis=dim)
        initial = lax.slice_in_dim(array, 0, width, axis=dim)
        before = lax.ppermute(last, axis, up)
        after = lax.ppermute(initial, axis, down)
        array = jnp.concatenate([before, array, after], axis=dim)
    return array


def derivatives(parts):
    first = (parts[0] - 8.0 * parts[1] + 8.0 * parts[3] - parts[4]) / 12.0
    second = (-parts[0] + 16.0 * parts[1] - 30.0 * parts[2] + 16.0 * parts[3] - parts[4]) / 12.0
    return (first, second)


def tendency(field):
    deep = padded(field, (("slab", 1),), 2, True)
    wide = padded(field, (("grp", 2),), 2, True)
    walls = padded(field, (("row", 3),), 2, False)
    depth, across, height = (field.shape[1], field.shape[2], field.shape[3])
    along_z = [deep[:, k : k + depth] for k in range(5)]
    along_x = [wide[:, :, k : k + across, :] for k in range(5)]
    along_y = [walls[:, :, :, k : k + height] for k in range(5)]
    dz_first, dz_second = derivatives(along_z)
    dx_first, dx_second = derivatives(along_x)
    dy_first, dy_second = derivatives(along_y)
    convect = field[0:1] * dx_first + field[1:2] * dy_first + field[2:3] * dz_first
    laplace = dx_second + dy_second + dz_second
    return viscosity * laplace - convect


def product(left, right, dims=((1,), (0,))):
    return lax.dot_general(
        left, right, (dims, ((), ())),
        precision=lax.Precision.HIGHEST, preferred_element_type=jnp.float32,
    )


def eliminate(tile, factor_ref, inverse_ref):
    size = tile.shape[0]
    lane = lax.broadcasted_iota(jnp.int32, (PANEL, size), 1)
    sub = lax.broadcasted_iota(jnp.int32, (PANEL, size), 0)
    groups = [tile[PANEL * g : PANEL * (g + 1), :] for g in range(size // PANEL)]
    for p in range(size // PANEL):
        start = PANEL * p
        own = groups[p]
        inside = (lane >= start) & (lane < start + PANEL)
        columns = [
            jnp.broadcast_to(own[:, start + k : start + k + 1], own.shape) for k in range(PANEL)
        ]
        direct = own
        unit = jnp.where(inside, jnp.where(lane - start == sub, 1.0, 0.0), own)
        factor_rows = jnp.zeros_like(own)
        inverse_rows = jnp.zeros_like(own)
        for k in range(PANEL):
            pivot = columns[k][k : k + 1, :]
            root = lax.rsqrt(pivot)
            scale = 1.0 / pivot
            here = sub == k
            row_direct, row_unit = direct[k : k + 1, :], unit[k : k + 1, :]
            factor_rows = jnp.where(here, row_direct * root, factor_rows)
            inverse_rows = jnp.where(here, row_unit * root, inverse_rows)
            others = jnp.where(here, 0.0, columns[k])
            for j in range(k + 1, PANEL):
                row = columns[j][k : k + 1, :] * scale
                columns[j] = jnp.where(here, row, columns[j]) - others * row
            row = row_direct * scale
            direct = jnp.where(here, row, direct) - others * row
            row = row_unit * scale
            unit = jnp.where(here, row, unit) - others * row
        factor_ref[start : start + PANEL, :] = jnp.where(lane >= start + sub, factor_rows, 0.0)
        inverse_ref[start : start + PANEL, :] = jnp.where(lane <= start + sub, inverse_rows, 0.0)
        for g in range(p + 1, size // PANEL):
            below = groups[g]
            total = jnp.where(inside, 0.0, below)
            for k in range(PANEL):
                total = total - below[:, start + k : start + k + 1] * unit[k : k + 1, :]
            groups[g] = total


def wire_stages():
    slab = (("slab",), lax.axis_size("slab"))
    rest = (("grp", "row"), lax.axis_size("grp") * lax.axis_size("row"))
    return [[slab, rest], [rest, slab]]


def place(stage):
    index = 0
    for axis in stage[0]:
        index = index * lax.axis_size(axis) + lax.axis_index(axis)
    return index


def peer(stage, distance):
    axes, members = stage
    other = lax.rem(place(stage) + distance, members)
    coords, left = {}, other
    for axis in reversed(axes):
        coords[axis] = lax.rem(left, lax.axis_size(axis))
        left = left // lax.axis_size(axis)
    return coords, other


def chunk_plan(rows, devices):
    unit = PANEL * devices
    units = rows // unit
    orders = wire_stages()
    chunks, base = [], 0
    for c in range(2):
        share = (units - base + 1 - c) // (2 - c)
        if share:
            chunks.append((base * unit, share, orders[c]))
            base += share
    return [(start, share * unit, order) for start, share, order in chunks]


def inbox_rows(chunks):
    total = 0
    for _, length, order in chunks:
        for _, members in order:
            length //= members
            total += (members - 1) * length
    return total


def wire_count(chunks):
    return 2 * sum(members - 1 for _, _, order in chunks for _, members in order)


def combine_kernel(chunks, swap, *refs):
    if swap:
        part_ref, mine_ref, sum_ref, got_ref, acc, full, inbox, send, recv, got, swap_send, swap_recv = refs
    else:
        part_ref, sum_ref, acc, full, inbox, send, recv = refs
    barrier = pltpu.get_barrier_semaphore()
    stages = chunks[0][2]
    slab = (("slab",), lax.axis_size("slab"))
    total = 0
    for stage in stages:
        for d in range(1, stage[1]):
            pl.semaphore_signal(barrier, inc=1, device_id=peer(stage, d)[0], device_id_type=pl.DeviceIdType.MESH)
            total += 1
    acc[...] = part_ref[...]
    pl.semaphore_wait(barrier, total)

    count = 0
    slot = 0
    pending = []

    def begin(source, target, device, index):
        copy = pltpu.make_async_remote_copy(
            src_ref=source, dst_ref=target, send_sem=send.at[index], recv_sem=recv.at[index],
            device_id=device, device_id_type=pl.DeviceIdType.MESH,
        )
        copy.start()
        pending.append(copy)
        return copy

    offsets = [jnp.int32(base) for base, _, _ in chunks]
    lengths = [length for _, length, _ in chunks]
    trail = [[] for _ in chunks]
    swaps = []
    for s in range(len(stages)):
        started = []
        for c, (_, _, order) in enumerate(chunks):
            stage = order[s]
            piece = lengths[c] // stage[1]
            for d in range(1, stage[1]):
                device, other = peer(stage, d)
                source = acc.at[pl.ds(pl.multiple_of(offsets[c] + other * piece, PANEL), piece), :]
                copy = begin(source, inbox.at[pl.ds(slot, piece), :], device, count)
                started.append((c, copy, slot, piece))
                count += 1
                slot += piece
        if swap and s == 0:
            me = lax.axis_index("slab")
            for d in range(1, slab[1]):
                device, other = peer(slab, d)
                copy = pltpu.make_async_remote_copy(
                    src_ref=mine_ref.at[other], dst_ref=got.at[me],
                    send_sem=swap_send.at[d - 1], recv_sem=swap_recv.at[d - 1],
                    device_id=device, device_id_type=pl.DeviceIdType.MESH,
                )
                copy.start()
                swaps.append(copy)
        for c, (_, _, order) in enumerate(chunks):
            stage = order[s]
            piece = lengths[c] // stage[1]
            trail[c].append((offsets[c], lengths[c]))
            offsets[c] = pl.multiple_of(offsets[c] + place(stage) * piece, PANEL)
            lengths[c] = piece
            rows = pl.ds(offsets[c], piece)
            for owner, copy, where, size in started:
                if owner == c:
                    copy.wait_recv()
                    acc[rows, :] = acc[rows, :] + inbox[pl.ds(where, size), :]
    for c in range(len(chunks)):
        rows = pl.ds(offsets[c], lengths[c])
        full[rows, :] = acc[rows, :]
    for s in reversed(range(len(stages))):
        started = []
        for c, (_, _, order) in enumerate(chunks):
            stage = order[s]
            rows = pl.ds(offsets[c], lengths[c])
            for d in range(1, stage[1]):
                started.append(begin(full.at[rows, :], full.at[rows, :], peer(stage, d)[0], count))
                count += 1
            offsets[c], lengths[c] = trail[c][s]
            offsets[c] = pl.multiple_of(offsets[c], PANEL)
        for copy in started:
            copy.wait_recv()
    sum_ref[...] = full[...]
    if swap:
        for copy in swaps:
            copy.wait_recv()
        for j in range(slab[1]):
            @pl.when(lax.axis_index("slab") == j)
            def _():
                got_ref[j] = mine_ref[j]

            @pl.when(lax.axis_index("slab") != j)
            def _():
                got_ref[j] = got[j]
    for copy in pending + swaps:
        copy.wait_send()


def combine(part, mine, collective_id):
    devices = lax.axis_size("grp") * lax.axis_size("slab") * lax.axis_size("row")
    chunks = chunk_plan(part.shape[0], devices)
    swap = mine is not None
    wires = wire_count(chunks)
    vmem = pl.BlockSpec(memory_space=pltpu.VMEM)
    out = [jax.ShapeDtypeStruct(part.shape, jnp.float32)]
    scratch = [
        pltpu.VMEM(part.shape, jnp.float32),
        pltpu.VMEM(part.shape, jnp.float32),
        pltpu.VMEM((inbox_rows(chunks), EDGE), jnp.float32),
        pltpu.SemaphoreType.DMA((wires,)),
        pltpu.SemaphoreType.DMA((wires,)),
    ]
    operands = [part]
    if swap:
        operands.append(mine)
        out.append(jax.ShapeDtypeStruct(mine.shape, jnp.float32))
        scratch += [
            pltpu.VMEM(mine.shape, jnp.float32),
            pltpu.SemaphoreType.DMA((mine.shape[0] - 1,)),
            pltpu.SemaphoreType.DMA((mine.shape[0] - 1,)),
        ]
    return pl.pallas_call(
        functools.partial(combine_kernel, chunks, swap),
        out_shape=out,
        in_specs=[vmem] * len(operands),
        out_specs=[vmem] * len(out),
        scratch_shapes=scratch,
        compiler_params=pltpu.CompilerParams(
            collective_id=collective_id, has_side_effects=True, vmem_limit_bytes=40 * 1024 * 1024
        ),
        name=f"combine_{collective_id}",
    )(*operands)


def round_up(value, unit):
    return -(-value // unit) * unit


def modes_gram_kernel(modes_ref, out_ref):
    blocks = modes_ref.shape[1] // EDGE
    at = 0
    for i in range(blocks):
        strip = product(modes_ref[:, i * EDGE : (i + 1) * EDGE], modes_ref[:, i * EDGE :], ((0,), (0,)))
        for j in range(blocks - i):
            out_ref[at : at + EDGE, :] = strip[:, j * EDGE : (j + 1) * EDGE]
            at += EDGE
    if at < out_ref.shape[0]:
        out_ref[at:, :] = jnp.zeros((out_ref.shape[0] - at, EDGE), jnp.float32)


def snapshot_gram_kernel(count, planes_ref, got_ref, modes_ref, rows_ref, out_ref):
    held = got_ref.shape[0]
    cells = lax.broadcasted_iota(jnp.int32, (EDGE, held), 1)
    chosen = jnp.where(cells == planes_ref[...], 1.0, 0.0)
    rows_ref[...] = product(chosen, got_ref[...])
    snapshots = rows_ref[...]
    blocks = modes_ref.shape[1] // EDGE
    cross = product(snapshots[:count, :], modes_ref[...])
    for i in range(blocks):
        out_ref[i * count : (i + 1) * count, :] = cross[:, i * EDGE : (i + 1) * EDGE]
    out_ref[blocks * count : (blocks + 1) * count, :] = product(snapshots[:count, :], snapshots, ((1,), (1,)))
    at = (blocks + 1) * count
    if at < out_ref.shape[0]:
        out_ref[at:, :] = jnp.zeros((out_ref.shape[0] - at, EDGE), jnp.float32)


def factor_kernel(count, rows_total, first_ref, second_ref, modes_ref, rows_ref, basis_ref, factor_ref,
                  work, left, tile, upper, lower):
    rank = modes_ref.shape[1]
    size = rank + count
    whole = work.shape[0]
    blocks = whole // EDGE
    scale = 1.0 / rows_total
    at = 0
    for i in range(blocks - 1):
        low = i * EDGE
        for j in range(i, blocks - 1):
            work[low : low + EDGE, j * EDGE : (j + 1) * EDGE] = first_ref[at : at + EDGE, :] * scale
            at += EDGE
        cross = jnp.concatenate(
            [second_ref[i * count : (i + 1) * count, :], jnp.zeros((EDGE - count, EDGE), jnp.float32)], axis=0
        )
        work[low : low + EDGE, rank:] = cross.T * scale
    row = lax.broadcasted_iota(jnp.int32, (EDGE, EDGE), 0)
    col = lax.broadcasted_iota(jnp.int32, (EDGE, EDGE), 1)
    inner = second_ref[(blocks - 1) * count : blocks * count, :] * scale
    work[rank : rank + count, rank:] = inner
    work[rank + count :, rank:] = jnp.where((row == col) & (row >= count), 1.0, 0.0)[count:, :]
    left[:, :rank] = modes_ref[...]
    left[:, rank:] = rows_ref[...].T
    factor_ref[...] = jnp.zeros_like(factor_ref)

    def step(k, carry):
        for b in range(blocks):
            @pl.when(k == b)
            def _():
                tile[...] = work[b * EDGE : (b + 1) * EDGE, b * EDGE : (b + 1) * EDGE]

        eliminate(tile[...], upper, lower)
        for b in range(blocks):
            @pl.when(k == b)
            def _():
                low, high = b * EDGE, (b + 1) * EDGE
                end = min(high, size)
                inverse = lower[...]
                solved = product(left[:, low:high], inverse, ((1,), (1,)))
                basis_ref[:, low:end] = solved[:, : end - low]
                factor_ref[low:end, low:end] = upper[: end - low, : end - low]
                if high < whole:
                    strip = product(inverse, work[low:high, high:])
                    factor_ref[low:high, high:] = strip[:, : size - high]
                    work[high:, high:] = work[high:, high:] - product(strip, strip, ((0,), (0,)))
                    left[:, high:] = left[:, high:] - product(solved, strip)

        return carry

    lax.fori_loop(0, blocks, step, 0)


def plain(kernel, out_shape, scratch, name, *operands):
    vmem = pl.BlockSpec(memory_space=pltpu.VMEM)
    shapes = [jax.ShapeDtypeStruct(shape, jnp.float32) for shape in out_shape]
    return pl.pallas_call(
        kernel,
        out_shape=shapes,
        in_specs=[vmem] * len(operands),
        out_specs=[vmem] * len(shapes),
        scratch_shapes=[pltpu.VMEM(shape, jnp.float32) for shape in scratch],
        compiler_params=pltpu.CompilerParams(vmem_limit_bytes=40 * 1024 * 1024),
        name=name,
    )(*operands)


def decompose(advanced, modes, planes, assign):
    count = planes.shape[0]
    slabs = lax.axis_size("slab")
    devices = lax.axis_size("grp") * slabs * lax.axis_size("row")
    rows, rank = modes.shape
    size = rank + count
    whole = rank + EDGE
    depth = advanced.shape[1]
    unit = PANEL * devices
    blocks = rank // EDGE
    (first,) = plain(modes_gram_kernel, [(round_up(blocks * (blocks + 1) // 2 * EDGE, unit), EDGE)], [],
                     "modes_gram", modes)
    pieces = jnp.transpose(advanced, (1, 0, 2, 3)).reshape(depth, slabs, -1)
    mine = jnp.transpose(jnp.take(pieces, assign, axis=1, mode="clip"), (1, 0, 2))
    first, got = combine(first, mine, 0)
    chosen = jnp.pad(planes, (0, EDGE - count), constant_values=-1).reshape(EDGE, 1)
    snapshots, second = plain(
        functools.partial(snapshot_gram_kernel, count),
        [(EDGE, rows), (round_up((blocks + 1) * count, unit), EDGE)], [], "snapshot_gram",
        chosen, got.reshape(slabs * depth, rows), modes,
    )
    (second,) = combine(second, None, 1)
    return plain(
        functools.partial(factor_kernel, count, float(rows * devices)),
        [(rows, size), (size, size)],
        [(whole, whole), (rows, whole), (EDGE, EDGE), (EDGE, EDGE), (EDGE, EDGE)],
        "factorize", first, second, modes, snapshots,
    )


def on_device(velocity, modes, planes, assign):
    first_q = step_size * tendency(velocity)
    middle = velocity + third * first_q
    second_q = carry_back * first_q + step_size * tendency(middle)
    advanced = middle + second_gain * second_q
    basis, factor = decompose(advanced, modes, planes, assign)
    return (advanced, basis, factor)


def solution(mesh):
    placed = (P(None, "slab", "grp", "row"), P(("grp", "slab", "row"), None), P(), P())
    return jax.shard_map(
        on_device,
        mesh=mesh,
        in_specs=placed,
        out_specs=(P(None, "slab", "grp", "row"), P(("grp", "slab", "row"), None), P()),
        check_vma=False,
    )
```

```python
import functools

import jax
import jax.numpy as jnp
from jax import lax
from jax.experimental import pallas as pl
from jax.experimental.pallas import tpu as pltpu
from jax.sharding import PartitionSpec as P

step_size = 0.05
viscosity = 1.0
third = 1.0 / 3.0
carry_back = -5.0 / 9.0
second_gain = 15.0 / 16.0
EDGE = 128
PANEL = 8


def padded(array, sides, width, wrap):
    for axis, dim in sides:
        devices, length = (lax.axis_size(axis), array.shape[dim])
        up = [(i, (i + 1) % devices) for i in range(devices if wrap else devices - 1)]
        down = [(j, i) for i, j in up]
        last = lax.slice_in_dim(array, length - width, length, axis=dim)
        initial = lax.slice_in_dim(array, 0, width, axis=dim)
        before = lax.ppermute(last, axis, up)
        after = lax.ppermute(initial, axis, down)
        array = jnp.concatenate([before, array, after], axis=dim)
    return array


def derivatives(parts):
    first = (parts[0] - 8.0 * parts[1] + 8.0 * parts[3] - parts[4]) / 12.0
    second = (-parts[0] + 16.0 * parts[1] - 30.0 * parts[2] + 16.0 * parts[3] - parts[4]) / 12.0
    return (first, second)


def tendency(field):
    deep = padded(field, (("slab", 1),), 2, True)
    wide = padded(field, (("grp", 2),), 2, True)
    walls = padded(field, (("row", 3),), 2, False)
    depth, across, height = (field.shape[1], field.shape[2], field.shape[3])
    along_z = [deep[:, k : k + depth] for k in range(5)]
    along_x = [wide[:, :, k : k + across, :] for k in range(5)]
    along_y = [walls[:, :, :, k : k + height] for k in range(5)]
    dz_first, dz_second = derivatives(along_z)
    dx_first, dx_second = derivatives(along_x)
    dy_first, dy_second = derivatives(along_y)
    convect = field[0:1] * dx_first + field[1:2] * dy_first + field[2:3] * dz_first
    laplace = dx_second + dy_second + dz_second
    return viscosity * laplace - convect


def product(left, right, dims=((1,), (0,))):
    return lax.dot_general(
        left, right, (dims, ((), ())),
        precision=lax.Precision.HIGHEST, preferred_element_type=jnp.float32,
    )


def eliminate(tile, factor_ref, inverse_ref):
    size = tile.shape[0]
    lane = lax.broadcasted_iota(jnp.int32, (PANEL, size), 1)
    sub = lax.broadcasted_iota(jnp.int32, (PANEL, size), 0)
    groups = [tile[PANEL * g : PANEL * (g + 1), :] for g in range(size // PANEL)]
    for p in range(size // PANEL):
        start = PANEL * p
        own = groups[p]
        inside = (lane >= start) & (lane < start + PANEL)
        columns = [
            jnp.broadcast_to(own[:, start + k : start + k + 1], own.shape) for k in range(PANEL)
        ]
        direct = own
        unit = jnp.where(inside, jnp.where(lane - start == sub, 1.0, 0.0), own)
        factor_rows = jnp.zeros_like(own)
        inverse_rows = jnp.zeros_like(own)
        for k in range(PANEL):
            pivot = columns[k][k : k + 1, :]
            root = lax.rsqrt(pivot)
            scale = 1.0 / pivot
            here = sub == k
            row_direct, row_unit = direct[k : k + 1, :], unit[k : k + 1, :]
            factor_rows = jnp.where(here, row_direct * root, factor_rows)
            inverse_rows = jnp.where(here, row_unit * root, inverse_rows)
            others = jnp.where(here, 0.0, columns[k])
            for j in range(k + 1, PANEL):
                row = columns[j][k : k + 1, :] * scale
                columns[j] = jnp.where(here, row, columns[j]) - others * row
            row = row_direct * scale
            direct = jnp.where(here, row, direct) - others * row
            row = row_unit * scale
            unit = jnp.where(here, row, unit) - others * row
        factor_ref[start : start + PANEL, :] = jnp.where(lane >= start + sub, factor_rows, 0.0)
        inverse_ref[start : start + PANEL, :] = jnp.where(lane <= start + sub, inverse_rows, 0.0)
        for g in range(p + 1, size // PANEL):
            below = groups[g]
            total = jnp.where(inside, 0.0, below)
            for k in range(PANEL):
                total = total - below[:, start + k : start + k + 1] * unit[k : k + 1, :]
            groups[g] = total


def wire_stages():
    slab = (("slab",), lax.axis_size("slab"))
    rest = (("grp", "row"), lax.axis_size("grp") * lax.axis_size("row"))
    return [[slab, rest], [rest, slab]]


def place(stage):
    index = 0
    for axis in stage[0]:
        index = index * lax.axis_size(axis) + lax.axis_index(axis)
    return index


def peer(stage, distance):
    axes, members = stage
    other = lax.rem(place(stage) + distance, members)
    coords, left = {}, other
    for axis in reversed(axes):
        coords[axis] = lax.rem(left, lax.axis_size(axis))
        left = left // lax.axis_size(axis)
    return coords, other


def chunk_plan(origin, rows, devices):
    unit = PANEL * devices
    units = rows // unit
    orders = wire_stages()
    chunks, base = [], 0
    for c in range(2):
        share = (units - base + 1 - c) // (2 - c)
        if share:
            chunks.append((base * unit, share, orders[c]))
            base += share
    return [(origin + start, share * unit, order) for start, share, order in chunks]


def inbox_rows(chunks):
    total = 0
    for _, length, order in chunks:
        for _, members in order:
            length //= members
            total += (members - 1) * length
    return total


def wire_count(chunks):
    return 2 * sum(members - 1 for _, _, order in chunks for _, members in order)


def combine_kernel(chunks, early, count, *refs):
    (part_ref, mine_ref, modes_ref, planes_ref, first_ref, second_ref, rows_ref,
     acc, full, inbox, send, recv, got, swap_send, swap_recv) = refs
    barrier = pltpu.get_barrier_semaphore()
    stages = chunks[0][2]
    deep = len(stages)
    slab = (("slab",), lax.axis_size("slab"))
    total = 0
    for stage in stages:
        for d in range(1, stage[1]):
            pl.semaphore_signal(barrier, inc=1, device_id=peer(stage, d)[0], device_id_type=pl.DeviceIdType.MESH)
            total += 1
    head = part_ref.shape[0]
    acc[:head, :] = part_ref[...]
    me = lax.axis_index("slab")
    for j in range(slab[1]):
        @pl.when(me == j)
        def _():
            got[j] = mine_ref[j]

    pl.semaphore_wait(barrier, total)

    used = [0, 0]
    pending = []

    def begin(source, target, device):
        copy = pltpu.make_async_remote_copy(
            src_ref=source, dst_ref=target, send_sem=send.at[used[0]], recv_sem=recv.at[used[0]],
            device_id=device, device_id_type=pl.DeviceIdType.MESH,
        )
        used[0] += 1
        copy.start()
        pending.append(copy)
        return copy

    offsets = [jnp.int32(base) for base, _, _ in chunks]
    lengths = [length for _, length, _ in chunks]
    trail = [[] for _ in chunks]

    def launch(c, phase):
        started = []
        if phase < deep:
            stage = chunks[c][2][phase]
            piece = lengths[c] // stage[1]
            for d in range(1, stage[1]):
                device, other = peer(stage, d)
                source = acc.at[pl.ds(pl.multiple_of(offsets[c] + other * piece, PANEL), piece), :]
                slot = used[1]
                started.append((begin(source, inbox.at[pl.ds(slot, piece), :], device), slot))
                used[1] += piece
            trail[c].append((offsets[c], lengths[c]))
            offsets[c] = pl.multiple_of(offsets[c] + place(stage) * piece, PANEL)
            lengths[c] = piece
        else:
            stage = chunks[c][2][2 * deep - 1 - phase]
            rows = pl.ds(offsets[c], lengths[c])
            if phase == deep:
                full[rows, :] = acc[rows, :]
            for d in range(1, stage[1]):
                started.append((begin(full.at[rows, :], full.at[rows, :], peer(stage, d)[0]), 0))
            offsets[c], lengths[c] = trail[c][2 * deep - 1 - phase]
            offsets[c] = pl.multiple_of(offsets[c], PANEL)
        return started

    def finish(c, phase, started):
        rows = pl.ds(offsets[c], lengths[c])
        for copy, slot in started:
            copy.wait_recv()
            if phase < deep:
                acc[rows, :] = acc[rows, :] + inbox[pl.ds(slot, lengths[c]), :]

    swaps = []
    for d in range(1, slab[1]):
        device, other = peer(slab, d)
        copy = pltpu.make_async_remote_copy(
            src_ref=mine_ref.at[other], dst_ref=got.at[me],
            send_sem=swap_send.at[d - 1], recv_sem=swap_recv.at[d - 1],
            device_id=device, device_id_type=pl.DeviceIdType.MESH,
        )
        copy.start()
        swaps.append(copy)
    late = range(early, len(chunks))
    for tick in range(2 * deep + 1):
        active = []
        if tick < 2 * deep:
            active += [(c, tick, launch(c, tick)) for c in range(early)]
        if tick == 1:
            for copy in swaps:
                copy.wait_recv()
            snapshot_gram(count, planes_ref, got, modes_ref, rows_ref, acc, head)
        if tick >= 1:
            active += [(c, tick - 1, launch(c, tick - 1)) for c in late]
        for c, phase, started in active:
            finish(c, phase, started)
    first_ref[...] = full[:head, :]
    second_ref[...] = full[head:, :]
    for copy in pending + swaps:
        copy.wait_send()


def combine(part, mine, modes, chosen, count):
    devices = lax.axis_size("grp") * lax.axis_size("slab") * lax.axis_size("row")
    head = part.shape[0]
    extra = round_up((modes.shape[1] // EDGE + 1) * count, PANEL * devices)
    first = chunk_plan(0, head, devices)
    chunks = first + chunk_plan(head, extra, devices)
    wires = wire_count(chunks)
    vmem = pl.BlockSpec(memory_space=pltpu.VMEM)
    shapes = [(head, EDGE), (extra, EDGE), (EDGE, modes.shape[0])]
    return pl.pallas_call(
        functools.partial(combine_kernel, chunks, len(first), count),
        out_shape=[jax.ShapeDtypeStruct(shape, jnp.float32) for shape in shapes],
        in_specs=[vmem] * 4,
        out_specs=[vmem] * 3,
        scratch_shapes=[
            pltpu.VMEM((head + extra, EDGE), jnp.float32),
            pltpu.VMEM((head + extra, EDGE), jnp.float32),
            pltpu.VMEM((inbox_rows(chunks), EDGE), jnp.float32),
            pltpu.SemaphoreType.DMA((wires,)),
            pltpu.SemaphoreType.DMA((wires,)),
            pltpu.VMEM(mine.shape, jnp.float32),
            pltpu.SemaphoreType.DMA((mine.shape[0] - 1,)),
            pltpu.SemaphoreType.DMA((mine.shape[0] - 1,)),
        ],
        compiler_params=pltpu.CompilerParams(
            collective_id=0, has_side_effects=True, vmem_limit_bytes=48 * 1024 * 1024
        ),
        name="combine",
    )(part, mine, modes, chosen)


def round_up(value, unit):
    return -(-value // unit) * unit


def modes_gram_kernel(modes_ref, out_ref):
    blocks = modes_ref.shape[1] // EDGE
    at = 0
    for i in range(blocks):
        strip = product(modes_ref[:, i * EDGE : (i + 1) * EDGE], modes_ref[:, i * EDGE :], ((0,), (0,)))
        for j in range(blocks - i):
            out_ref[at : at + EDGE, :] = strip[:, j * EDGE : (j + 1) * EDGE]
            at += EDGE
    if at < out_ref.shape[0]:
        out_ref[at:, :] = jnp.zeros((out_ref.shape[0] - at, EDGE), jnp.float32)


def snapshot_gram(count, planes_ref, got_ref, modes_ref, rows_ref, out_ref, base):
    slabs, depth = got_ref.shape[0], got_ref.shape[1]
    cells = lax.broadcasted_iota(jnp.int32, (EDGE, slabs * depth), 1)
    chosen = jnp.where(cells == planes_ref[...], 1.0, 0.0)
    held = got_ref[...].reshape(slabs * depth, got_ref.shape[2])
    snapshots = product(chosen, held)
    rows_ref[...] = snapshots
    blocks = modes_ref.shape[1] // EDGE
    cross = product(snapshots[:count, :], modes_ref[...])
    for i in range(blocks):
        out_ref[base + i * count : base + (i + 1) * count, :] = cross[:, i * EDGE : (i + 1) * EDGE]
    at = base + blocks * count
    out_ref[at : at + count, :] = product(snapshots[:count, :], snapshots, ((1,), (1,)))
    at += count
    if at < out_ref.shape[0]:
        out_ref[at:, :] = jnp.zeros((out_ref.shape[0] - at, EDGE), jnp.float32)


def factor_kernel(count, rows_total, first_ref, second_ref, modes_ref, rows_ref, basis_ref, factor_ref,
                  work, left, tile, upper, lower):
    rank = modes_ref.shape[1]
    size = rank + count
    whole = work.shape[0]
    blocks = whole // EDGE
    scale = 1.0 / rows_total
    at = 0
    for i in range(blocks - 1):
        low = i * EDGE
        for j in range(i, blocks - 1):
            work[low : low + EDGE, j * EDGE : (j + 1) * EDGE] = first_ref[at : at + EDGE, :] * scale
            at += EDGE
        cross = jnp.concatenate(
            [second_ref[i * count : (i + 1) * count, :], jnp.zeros((EDGE - count, EDGE), jnp.float32)], axis=0
        )
        work[low : low + EDGE, rank:] = cross.T * scale
    row = lax.broadcasted_iota(jnp.int32, (EDGE, EDGE), 0)
    col = lax.broadcasted_iota(jnp.int32, (EDGE, EDGE), 1)
    inner = second_ref[(blocks - 1) * count : blocks * count, :] * scale
    work[rank : rank + count, rank:] = inner
    work[rank + count :, rank:] = jnp.where((row == col) & (row >= count), 1.0, 0.0)[count:, :]
    left[:, :rank] = modes_ref[...]
    left[:, rank:] = rows_ref[...].T
    factor_ref[...] = jnp.zeros_like(factor_ref)

    def step(k, carry):
        for b in range(blocks):
            @pl.when(k == b)
            def _():
                tile[...] = work[b * EDGE : (b + 1) * EDGE, b * EDGE : (b + 1) * EDGE]

        eliminate(tile[...], upper, lower)
        for b in range(blocks):
            @pl.when(k == b)
            def _():
                low, high = b * EDGE, (b + 1) * EDGE
                end = min(high, size)
                inverse = lower[...]
                solved = product(left[:, low:high], inverse, ((1,), (1,)))
                basis_ref[:, low:end] = solved[:, : end - low]
                factor_ref[low:end, low:end] = upper[: end - low, : end - low]
                if high < whole:
                    strip = product(inverse, work[low:high, high:])
                    factor_ref[low:high, high:] = strip[:, : size - high]
                    work[high:, high:] = work[high:, high:] - product(strip, strip, ((0,), (0,)))
                    left[:, high:] = left[:, high:] - product(solved, strip)

        return carry

    lax.fori_loop(0, blocks, step, 0)


def plain(kernel, out_shape, scratch, name, *operands):
    vmem = pl.BlockSpec(memory_space=pltpu.VMEM)
    shapes = [jax.ShapeDtypeStruct(shape, jnp.float32) for shape in out_shape]
    return pl.pallas_call(
        kernel,
        out_shape=shapes,
        in_specs=[vmem] * len(operands),
        out_specs=[vmem] * len(shapes),
        scratch_shapes=[pltpu.VMEM(shape, jnp.float32) for shape in scratch],
        compiler_params=pltpu.CompilerParams(vmem_limit_bytes=40 * 1024 * 1024),
        name=name,
    )(*operands)


def decompose(advanced, modes, planes, assign):
    count = planes.shape[0]
    slabs = lax.axis_size("slab")
    devices = lax.axis_size("grp") * slabs * lax.axis_size("row")
    rows, rank = modes.shape
    size = rank + count
    whole = rank + EDGE
    depth = advanced.shape[1]
    unit = PANEL * devices
    blocks = rank // EDGE
    (first,) = plain(modes_gram_kernel, [(round_up(blocks * (blocks + 1) // 2 * EDGE, unit), EDGE)], [],
                     "modes_gram", modes)
    pieces = jnp.transpose(advanced, (1, 0, 2, 3)).reshape(depth, slabs, -1)
    mine = jnp.transpose(jnp.take(pieces, assign, axis=1, mode="clip"), (1, 0, 2))
    chosen = jnp.pad(planes, (0, EDGE - count), constant_values=-1).reshape(EDGE, 1)
    first, second, snapshots = combine(first, mine, modes, chosen, count)
    return plain(
        functools.partial(factor_kernel, count, float(rows * devices)),
        [(rows, size), (size, size)],
        [(whole, whole), (rows, whole), (EDGE, EDGE), (EDGE, EDGE), (EDGE, EDGE)],
        "factorize", first, second, modes, snapshots,
    )


def on_device(velocity, modes, planes, assign):
    first_q = step_size * tendency(velocity)
    middle = velocity + third * first_q
    second_q = carry_back * first_q + step_size * tendency(middle)
    advanced = middle + second_gain * second_q
    basis, factor = decompose(advanced, modes, planes, assign)
    return (advanced, basis, factor)


def solution(mesh):
    placed = (P(None, "slab", "grp", "row"), P(("grp", "slab", "row"), None), P(), P())
    return jax.shard_map(
        on_device,
        mesh=mesh,
        in_specs=placed,
        out_specs=(P(None, "slab", "grp", "row"), P(("grp", "slab", "row"), None), P()),
        check_vma=False,
    )
```

```python
import functools

import jax
import jax.numpy as jnp
from jax import lax
from jax.experimental import pallas as pl
from jax.experimental.pallas import tpu as pltpu
from jax.sharding import PartitionSpec as P

step_size = 0.05
viscosity = 1.0
third = 1.0 / 3.0
carry_back = -5.0 / 9.0
second_gain = 15.0 / 16.0
EDGE = 128
PANEL = 8


def padded(array, sides, width, wrap):
    for axis, dim in sides:
        devices, length = (lax.axis_size(axis), array.shape[dim])
        up = [(i, (i + 1) % devices) for i in range(devices if wrap else devices - 1)]
        down = [(j, i) for i, j in up]
        last = lax.slice_in_dim(array, length - width, length, axis=dim)
        initial = lax.slice_in_dim(array, 0, width, axis=dim)
        if dim == array.ndim - 1:
            shape = (width,) + array.shape[:-1]
            last = jnp.moveaxis(last, -1, 0).reshape(width, -1)
            initial = jnp.moveaxis(initial, -1, 0).reshape(width, -1)
        before = lax.ppermute(last, axis, up)
        after = lax.ppermute(initial, axis, down)
        if dim == array.ndim - 1:
            before = jnp.moveaxis(before.reshape(shape), 0, -1)
            after = jnp.moveaxis(after.reshape(shape), 0, -1)
        array = jnp.concatenate([before, array, after], axis=dim)
    return array


def derivatives(parts):
    first = (parts[0] - 8.0 * parts[1] + 8.0 * parts[3] - parts[4]) / 12.0
    second = (-parts[0] + 16.0 * parts[1] - 30.0 * parts[2] + 16.0 * parts[3] - parts[4]) / 12.0
    return (first, second)


def tendency(field):
    deep = padded(field, (("slab", 1),), 2, True)
    wide = padded(field, (("grp", 2),), 2, True)
    walls = padded(field, (("row", 3),), 2, False)
    depth, across, height = (field.shape[1], field.shape[2], field.shape[3])
    along_z = [deep[:, k : k + depth] for k in range(5)]
    along_x = [wide[:, :, k : k + across, :] for k in range(5)]
    along_y = [walls[:, :, :, k : k + height] for k in range(5)]
    dz_first, dz_second = derivatives(along_z)
    dx_first, dx_second = derivatives(along_x)
    dy_first, dy_second = derivatives(along_y)
    convect = field[0:1] * dx_first + field[1:2] * dy_first + field[2:3] * dz_first
    laplace = dx_second + dy_second + dz_second
    return viscosity * laplace - convect


def product(left, right, dims=((1,), (0,))):
    return lax.dot_general(
        left, right, (dims, ((), ())),
        precision=lax.Precision.HIGHEST, preferred_element_type=jnp.float32,
    )


def eliminate(tile, factor_ref, inverse_ref):
    size = tile.shape[0]
    lane = lax.broadcasted_iota(jnp.int32, (PANEL, size), 1)
    sub = lax.broadcasted_iota(jnp.int32, (PANEL, size), 0)
    groups = [tile[PANEL * g : PANEL * (g + 1), :] for g in range(size // PANEL)]
    for p in range(size // PANEL):
        start = PANEL * p
        own = groups[p]
        inside = (lane >= start) & (lane < start + PANEL)
        columns = [
            jnp.broadcast_to(own[:, start + k : start + k + 1], own.shape) for k in range(PANEL)
        ]
        direct = own
        unit = jnp.where(inside, jnp.where(lane - start == sub, 1.0, 0.0), own)
        factor_rows = jnp.zeros_like(own)
        inverse_rows = jnp.zeros_like(own)
        for k in range(PANEL):
            pivot = columns[k][k : k + 1, :]
            root = lax.rsqrt(pivot)
            scale = 1.0 / pivot
            here = sub == k
            row_direct, row_unit = direct[k : k + 1, :], unit[k : k + 1, :]
            factor_rows = jnp.where(here, row_direct * root, factor_rows)
            inverse_rows = jnp.where(here, row_unit * root, inverse_rows)
            others = jnp.where(here, 0.0, columns[k])
            for j in range(k + 1, PANEL):
                row = columns[j][k : k + 1, :] * scale
                columns[j] = jnp.where(here, row, columns[j]) - others * row
            row = row_direct * scale
            direct = jnp.where(here, row, direct) - others * row
            row = row_unit * scale
            unit = jnp.where(here, row, unit) - others * row
        factor_ref[start : start + PANEL, :] = jnp.where(lane >= start + sub, factor_rows, 0.0)
        inverse_ref[start : start + PANEL, :] = jnp.where(lane <= start + sub, inverse_rows, 0.0)
        for g in range(p + 1, size // PANEL):
            below = groups[g]
            total = jnp.where(inside, 0.0, below)
            for k in range(PANEL):
                total = total - below[:, start + k : start + k + 1] * unit[k : k + 1, :]
            groups[g] = total


def wire_stages():
    slab = (("slab",), lax.axis_size("slab"))
    rest = (("grp", "row"), lax.axis_size("grp") * lax.axis_size("row"))
    return [[slab, rest], [rest, slab]]


def place(stage):
    index = 0
    for axis in stage[0]:
        index = index * lax.axis_size(axis) + lax.axis_index(axis)
    return index


def peer(stage, distance):
    axes, members = stage
    other = lax.rem(place(stage) + distance, members)
    coords, left = {}, other
    for axis in reversed(axes):
        coords[axis] = lax.rem(left, lax.axis_size(axis))
        left = left // lax.axis_size(axis)
    return coords, other


def chunk_plan(origin, rows, devices):
    unit = PANEL * devices
    units = rows // unit
    orders = wire_stages()
    chunks, base = [], 0
    for c in range(2):
        share = (units - base + 1 - c) // (2 - c)
        if share:
            chunks.append((base * unit, share, orders[c]))
            base += share
    return [(origin + start, share * unit, order) for start, share, order in chunks]


def inbox_rows(chunks):
    total = 0
    for _, length, order in chunks:
        for _, members in order:
            length //= members
            total += (members - 1) * length
    return total


def wire_count(chunks):
    return 2 * sum(members - 1 for _, _, order in chunks for _, members in order)


def combine_kernel(chunks, early, count, *refs):
    (part_ref, mine_ref, modes_ref, planes_ref, first_ref, second_ref, rows_ref,
     acc, full, inbox, send, recv, got, swap_send, swap_recv) = refs
    barrier = pltpu.get_barrier_semaphore()
    stages = chunks[0][2]
    deep = len(stages)
    slab = (("slab",), lax.axis_size("slab"))
    total = 0
    for stage in stages:
        for d in range(1, stage[1]):
            pl.semaphore_signal(barrier, inc=1, device_id=peer(stage, d)[0], device_id_type=pl.DeviceIdType.MESH)
            total += 1
    head = part_ref.shape[0]
    acc[:head, :] = part_ref[...]
    me = lax.axis_index("slab")
    for j in range(slab[1]):
        @pl.when(me == j)
        def _():
            got[j] = mine_ref[j]

    pl.semaphore_wait(barrier, total)

    used = [0, 0]
    pending = []

    def begin(source, target, device):
        copy = pltpu.make_async_remote_copy(
            src_ref=source, dst_ref=target, send_sem=send.at[used[0]], recv_sem=recv.at[used[0]],
            device_id=device, device_id_type=pl.DeviceIdType.MESH,
        )
        used[0] += 1
        copy.start()
        pending.append(copy)
        return copy

    offsets = [jnp.int32(base) for base, _, _ in chunks]
    lengths = [length for _, length, _ in chunks]
    trail = [[] for _ in chunks]

    def launch(c, phase):
        started = []
        if phase < deep:
            stage = chunks[c][2][phase]
            piece = lengths[c] // stage[1]
            for d in range(1, stage[1]):
                device, other = peer(stage, d)
                source = acc.at[pl.ds(pl.multiple_of(offsets[c] + other * piece, PANEL), piece), :]
                slot = used[1]
                started.append((begin(source, inbox.at[pl.ds(slot, piece), :], device), slot))
                used[1] += piece
            trail[c].append((offsets[c], lengths[c]))
            offsets[c] = pl.multiple_of(offsets[c] + place(stage) * piece, PANEL)
            lengths[c] = piece
        else:
            stage = chunks[c][2][2 * deep - 1 - phase]
            rows = pl.ds(offsets[c], lengths[c])
            if phase == deep:
                full[rows, :] = acc[rows, :]
            for d in range(1, stage[1]):
                started.append((begin(full.at[rows, :], full.at[rows, :], peer(stage, d)[0]), 0))
            offsets[c], lengths[c] = trail[c][2 * deep - 1 - phase]
            offsets[c] = pl.multiple_of(offsets[c], PANEL)
        return started

    def finish(c, phase, started):
        rows = pl.ds(offsets[c], lengths[c])
        for copy, slot in started:
            copy.wait_recv()
            if phase < deep:
                acc[rows, :] = acc[rows, :] + inbox[pl.ds(slot, lengths[c]), :]

    swaps = []
    for d in range(1, slab[1]):
        device, other = peer(slab, d)
        copy = pltpu.make_async_remote_copy(
            src_ref=mine_ref.at[other], dst_ref=got.at[me],
            send_sem=swap_send.at[d - 1], recv_sem=swap_recv.at[d - 1],
            device_id=device, device_id_type=pl.DeviceIdType.MESH,
        )
        copy.start()
        swaps.append(copy)
    late = range(early, len(chunks))
    for tick in range(2 * deep + 1):
        active = []
        if tick < 2 * deep:
            active += [(c, tick, launch(c, tick)) for c in range(early)]
        if tick == 1:
            for copy in swaps:
                copy.wait_recv()
            snapshot_gram(count, planes_ref, got, modes_ref, rows_ref, acc, head)
        if tick >= 1:
            active += [(c, tick - 1, launch(c, tick - 1)) for c in late]
        for c, phase, started in active:
            finish(c, phase, started)
    first_ref[...] = full[:head, :]
    second_ref[...] = full[head:, :]
    for copy in pending + swaps:
        copy.wait_send()


def combine(part, mine, modes, chosen, count):
    devices = lax.axis_size("grp") * lax.axis_size("slab") * lax.axis_size("row")
    head = part.shape[0]
    extra = round_up((modes.shape[1] // EDGE + 1) * count, PANEL * devices)
    first = chunk_plan(0, head, devices)
    chunks = first + chunk_plan(head, extra, devices)
    wires = wire_count(chunks)
    vmem = pl.BlockSpec(memory_space=pltpu.VMEM)
    shapes = [(head, EDGE), (extra, EDGE), (EDGE, modes.shape[0])]
    return pl.pallas_call(
        functools.partial(combine_kernel, chunks, len(first), count),
        out_shape=[jax.ShapeDtypeStruct(shape, jnp.float32) for shape in shapes],
        in_specs=[vmem] * 4,
        out_specs=[vmem] * 3,
        scratch_shapes=[
            pltpu.VMEM((head + extra, EDGE), jnp.float32),
            pltpu.VMEM((head + extra, EDGE), jnp.float32),
            pltpu.VMEM((inbox_rows(chunks), EDGE), jnp.float32),
            pltpu.SemaphoreType.DMA((wires,)),
            pltpu.SemaphoreType.DMA((wires,)),
            pltpu.VMEM(mine.shape, jnp.float32),
            pltpu.SemaphoreType.DMA((mine.shape[0] - 1,)),
            pltpu.SemaphoreType.DMA((mine.shape[0] - 1,)),
        ],
        compiler_params=pltpu.CompilerParams(
            collective_id=0, has_side_effects=True, vmem_limit_bytes=48 * 1024 * 1024
        ),
        name="combine",
    )(part, mine, modes, chosen)


def round_up(value, unit):
    return -(-value // unit) * unit


def modes_gram_kernel(modes_ref, out_ref):
    blocks = modes_ref.shape[1] // EDGE
    at = 0
    for i in range(blocks):
        strip = product(modes_ref[:, i * EDGE : (i + 1) * EDGE], modes_ref[:, i * EDGE :], ((0,), (0,)))
        for j in range(blocks - i):
            out_ref[at : at + EDGE, :] = strip[:, j * EDGE : (j + 1) * EDGE]
            at += EDGE
    if at < out_ref.shape[0]:
        out_ref[at:, :] = jnp.zeros((out_ref.shape[0] - at, EDGE), jnp.float32)


def snapshot_gram(count, planes_ref, got_ref, modes_ref, rows_ref, out_ref, base):
    slabs, depth = got_ref.shape[0], got_ref.shape[1]
    cells = lax.broadcasted_iota(jnp.int32, (EDGE, slabs * depth), 1)
    chosen = jnp.where(cells == planes_ref[...], 1.0, 0.0)
    held = got_ref[...].reshape(slabs * depth, got_ref.shape[2])
    snapshots = product(chosen, held)
    rows_ref[...] = snapshots
    blocks = modes_ref.shape[1] // EDGE
    cross = product(snapshots[:count, :], modes_ref[...])
    for i in range(blocks):
        out_ref[base + i * count : base + (i + 1) * count, :] = cross[:, i * EDGE : (i + 1) * EDGE]
    at = base + blocks * count
    out_ref[at : at + count, :] = product(snapshots[:count, :], snapshots, ((1,), (1,)))
    at += count
    if at < out_ref.shape[0]:
        out_ref[at:, :] = jnp.zeros((out_ref.shape[0] - at, EDGE), jnp.float32)


def factor_kernel(count, rows_total, first_ref, second_ref, modes_ref, rows_ref, basis_ref, factor_ref,
                  work, left, tile, upper, lower):
    rank = modes_ref.shape[1]
    size = rank + count
    whole = work.shape[0]
    blocks = whole // EDGE
    scale = 1.0 / rows_total
    at = 0
    for i in range(blocks - 1):
        low = i * EDGE
        for j in range(i, blocks - 1):
            work[low : low + EDGE, j * EDGE : (j + 1) * EDGE] = first_ref[at : at + EDGE, :] * scale
            at += EDGE
        cross = jnp.concatenate(
            [second_ref[i * count : (i + 1) * count, :], jnp.zeros((EDGE - count, EDGE), jnp.float32)], axis=0
        )
        work[low : low + EDGE, rank:] = cross.T * scale
    row = lax.broadcasted_iota(jnp.int32, (EDGE, EDGE), 0)
    col = lax.broadcasted_iota(jnp.int32, (EDGE, EDGE), 1)
    inner = second_ref[(blocks - 1) * count : blocks * count, :] * scale
    work[rank : rank + count, rank:] = inner
    work[rank + count :, rank:] = jnp.where((row == col) & (row >= count), 1.0, 0.0)[count:, :]
    left[:, :rank] = modes_ref[...]
    left[:, rank:] = rows_ref[...].T
    factor_ref[...] = jnp.zeros_like(factor_ref)

    def step(k, carry):
        for b in range(blocks):
            @pl.when(k == b)
            def _():
                tile[...] = work[b * EDGE : (b + 1) * EDGE, b * EDGE : (b + 1) * EDGE]

        eliminate(tile[...], upper, lower)
        for b in range(blocks):
            @pl.when(k == b)
            def _():
                low, high = b * EDGE, (b + 1) * EDGE
                end = min(high, size)
                inverse = lower[...]
                solved = product(left[:, low:high], inverse, ((1,), (1,)))
                basis_ref[:, low:end] = solved[:, : end - low]
                factor_ref[low:end, low:end] = upper[: end - low, : end - low]
                if high < whole:
                    strip = product(inverse, work[low:high, high:])
                    factor_ref[low:high, high:] = strip[:, : size - high]
                    work[high:, high:] = work[high:, high:] - product(strip, strip, ((0,), (0,)))
                    left[:, high:] = left[:, high:] - product(solved, strip)

        return carry

    lax.fori_loop(0, blocks, step, 0)


def plain(kernel, out_shape, scratch, name, *operands):
    vmem = pl.BlockSpec(memory_space=pltpu.VMEM)
    shapes = [jax.ShapeDtypeStruct(shape, jnp.float32) for shape in out_shape]
    return pl.pallas_call(
        kernel,
        out_shape=shapes,
        in_specs=[vmem] * len(operands),
        out_specs=[vmem] * len(shapes),
        scratch_shapes=[pltpu.VMEM(shape, jnp.float32) for shape in scratch],
        compiler_params=pltpu.CompilerParams(vmem_limit_bytes=40 * 1024 * 1024),
        name=name,
    )(*operands)


def decompose(advanced, modes, planes, assign):
    count = planes.shape[0]
    slabs = lax.axis_size("slab")
    devices = lax.axis_size("grp") * slabs * lax.axis_size("row")
    rows, rank = modes.shape
    size = rank + count
    whole = rank + EDGE
    depth = advanced.shape[1]
    unit = PANEL * devices
    blocks = rank // EDGE
    (first,) = plain(modes_gram_kernel, [(round_up(blocks * (blocks + 1) // 2 * EDGE, unit), EDGE)], [],
                     "modes_gram", modes)
    pieces = jnp.transpose(advanced, (1, 0, 2, 3)).reshape(depth, slabs, -1)
    mine = jnp.transpose(jnp.take(pieces, assign, axis=1, mode="clip"), (1, 0, 2))
    chosen = jnp.pad(planes, (0, EDGE - count), constant_values=-1).reshape(EDGE, 1)
    first, second, snapshots = combine(first, mine, modes, chosen, count)
    return plain(
        functools.partial(factor_kernel, count, float(rows * devices)),
        [(rows, size), (size, size)],
        [(whole, whole), (rows, whole), (EDGE, EDGE), (EDGE, EDGE), (EDGE, EDGE)],
        "factorize", first, second, modes, snapshots,
    )


def on_device(velocity, modes, planes, assign):
    first_q = step_size * tendency(velocity)
    middle = velocity + third * first_q
    second_q = carry_back * first_q + step_size * tendency(middle)
    advanced = middle + second_gain * second_q
    basis, factor = decompose(advanced, modes, planes, assign)
    return (advanced, basis, factor)


def solution(mesh):
    placed = (P(None, "slab", "grp", "row"), P(("grp", "slab", "row"), None), P(), P())
    return jax.shard_map(
        on_device,
        mesh=mesh,
        in_specs=placed,
        out_specs=(P(None, "slab", "grp", "row"), P(("grp", "slab", "row"), None), P()),
        check_vma=False,
    )
```
